32 devices in a mesh: blk: 1, dev: 32 (over z, y, x, core).
Axes of the slice: x: 2, y: 2, z: 4, core: 2. Of those that a mesh axis runs over, the one named last changes fastest.
Arguments:
- echoes: bfloat16 [2, 4, 256, 16384], P(None, None, ('blk', 'dev')), may hold values from -6 to 6
- range_phase: float32 [16384], replicated, may hold values from -3.140625 to 3.140625
- offsets: int32 [16384], P('dev'), may hold values from 0 to 56, as said below
- tap_weights: float32 [8, 384], replicated, may hold values from -2 to 2
- channel_mix: float32 [2, 4, 4, 384], replicated, may hold values from -2 to 2
- azimuth_filter: float32 [2, 4, 384], replicated, may hold values from -4 to 4
Outputs:
- focused_image: bfloat16 [2, 4, 256, 16384], P(None, None, 'blk', 'dev')
The draws below stay inside these ranges and needn't reach their ends.
Inputs may be any that keep to these rules, and one draw needn't show every extreme that they name: `offsets`: each range bin's offset lies between 0 and 56; some range bin has exactly 56.
All inputs are finite; a program needn't handle non-finite values.
Results may differ from the reference program's by a relative error of at most 0.0088.
Values may be sent and summed in bfloat16 or wider, within the bound.
A program may use at most 128 MiB of HBM per device.

```python
import math
import jax
import jax.numpy as jnp
from jax import lax

NR = 16384
R1 = 128
R2 = 128
CH = 4
TAPS = 8
MARG = 64
GROUP_P = 256
INTERSECTION = 128
WINDOW = 384
PULSES = 256
N_BLK = 1


def draw_offsets(key, part):
    values = jax.random.randint(jax.random.fold_in(key, 11), (NR,), 0, MARG - TAPS + 1)
    spots = jax.random.randint(jax.random.fold_in(key, 12), (2,), 0, NR)
    values = values.at[spots[0]].set(0)
    values = values.at[spots[1]].set(MARG - TAPS)
    return values.astype(jnp.int32)


def shard_levels(stream_key, extent, shards, low, top_value):
    def one(dim, shards_of):
        draws = jax.random.uniform(jax.random.fold_in(jax.random.fold_in(stream_key, 6), dim), (shards_of,), jnp.float32, low / len(shards), top_value / len(shards))
        return jnp.repeat(jnp.exp(draws), extent[dim] // shards_of).reshape((-1,) + (1,) * (len(extent) - dim - 1))

    gain = one(*shards[0])
    for cut in shards[1:]:
        gain = gain * one(*cut)
    return gain


def scatter_about(stream_key, dims, spread, limit, cuts=(), held_as=jnp.bfloat16):
    result = jax.random.normal(stream_key, dims, jnp.float32) * spread
    if len(cuts) > 0:
        result = shard_levels(stream_key, dims, cuts, -0.22, 0.18) * result
    return jnp.clip(result, min=-limit, max=limit).astype(held_as)


def setup_inputs(seed: int = 0) -> dict:
    seeds = jax.random.split(jax.random.key(seed), 7)
    echoes = scatter_about(seeds[0], (2, CH, PULSES, NR), 1.0, 6.0, ((2, 32),))
    range_phase = jnp.clip(jax.random.uniform(seeds[1], (NR,), jnp.float32, -3.140625, 3.140625), -3.140625, 3.140625)
    offsets = draw_offsets(jax.random.fold_in(seeds[6], 71), 0)
    tap_weights = scatter_about(seeds[3], (TAPS, WINDOW), TAPS ** -0.5, 2.0, (), jnp.float32)
    channel_mix = scatter_about(seeds[4], (2, CH, CH, WINDOW), 0.35, 2.0, (), jnp.float32)
    azimuth_filter = scatter_about(seeds[5], (2, CH, WINDOW), 0.7, 4.0, (), jnp.float32)
    return dict(echoes=echoes, range_phase=range_phase, offsets=offsets, tap_weights=tap_weights, channel_mix=channel_mix, azimuth_filter=azimuth_filter)


def phase_pair(row_count, col_count, length, direction, factor):
    product = jnp.arange(row_count, dtype=jnp.int32)[:, None] * jnp.arange(col_count, dtype=jnp.int32)[None, :] % length
    angle = product.astype(jnp.float32) * (direction * 2.0 * math.pi / length)
    return (jnp.cos(angle) * factor, jnp.sin(angle) * factor)

def settle(values):
    return lax.optimization_barrier(values.astype(jnp.bfloat16)).astype(jnp.float32)

def rounded_pair(row_count, col_count, length, direction, factor):
    cosine, sine = phase_pair(row_count, col_count, length, direction, factor)
    return (settle(cosine), settle(sine))

def compress(echo, range_phase):
    cosine = jnp.cos(range_phase)
    sine = jnp.sin(range_phase)
    real_in = echo[0].astype(jnp.float32)
    imag_in = echo[1].astype(jnp.float32)
    spec_real = settle(real_in * cosine - imag_in * sine)
    spec_imag = settle(real_in * sine + imag_in * cosine)
    leading_shape = spec_real.shape[:-1]
    spec_real = spec_real.reshape(leading_shape + (R1, R2))
    spec_imag = spec_imag.reshape(leading_shape + (R1, R2))
    first_re, first_im = rounded_pair(R1, R1, R1, 1.0, 1.0)
    section_real = jnp.einsum('nj,cqjb->cqnb', first_re, spec_real) - jnp.einsum('nj,cqjb->cqnb', first_im, spec_imag)
    section_imag = jnp.einsum('nj,cqjb->cqnb', first_re, spec_imag) + jnp.einsum('nj,cqjb->cqnb', first_im, spec_real)
    twist_re, twist_im = phase_pair(R1, R2, NR, 1.0, 1.0 / math.sqrt(NR))
    part_real = settle(section_real * twist_re - section_imag * twist_im)
    part_imag = settle(section_real * twist_im + section_imag * twist_re)
    second_re, second_im = rounded_pair(R2, R2, R2, 1.0, 1.0)
    out_real = jnp.einsum('cqnb,bm->cqmn', part_real, second_re) - jnp.einsum('cqnb,bm->cqmn', part_imag, second_im)
    out_imag = jnp.einsum('cqnb,bm->cqmn', part_real, second_im) + jnp.einsum('cqnb,bm->cqmn', part_imag, second_re)
    return jnp.stack([out_real, out_imag]).reshape((2,) + leading_shape + (NR,)).astype(jnp.bfloat16)

def focus(window, offsets, tap_weights, channel_mix, azimuth_filter):
    fwd_re, fwd_im = rounded_pair(WINDOW, WINDOW, WINDOW, -1.0, 1.0 / math.sqrt(WINDOW))
    win_real = window[0].astype(jnp.float32)
    win_imag = window[1].astype(jnp.float32)
    dop_real = jnp.einsum('fw,cwr->crf', fwd_re, win_real) - jnp.einsum('fw,cwr->crf', fwd_im, win_imag)
    dop_imag = jnp.einsum('fw,cwr->crf', fwd_re, win_imag) + jnp.einsum('fw,cwr->crf', fwd_im, win_real)
    dop_real = settle(dop_real)
    dop_imag = settle(dop_imag)
    tail = jnp.zeros((CH, MARG, WINDOW), jnp.float32)
    ext_real = jnp.concatenate([dop_real, tail], axis=1)
    ext_imag = jnp.concatenate([dop_imag, tail], axis=1)
    moved_real = jnp.zeros((CH, NR, WINDOW), jnp.float32)
    moved_imag = jnp.zeros((CH, NR, WINDOW), jnp.float32)
    start_rows = jnp.arange(NR, dtype=jnp.int32) + offsets.astype(jnp.int32)
    for tap_index in range(TAPS):
        chosen = (start_rows + tap_index).astype(jnp.int32)
        moved_real = moved_real + jnp.take(ext_real, chosen, axis=1) * tap_weights[tap_index]
        moved_imag = moved_imag + jnp.take(ext_imag, chosen, axis=1) * tap_weights[tap_index]
    rows_real = []
    rows_imag = []
    for channel in range(CH):
        sum_real = jnp.zeros((NR, WINDOW), jnp.float32)
        sum_imag = jnp.zeros((NR, WINDOW), jnp.float32)
        for other_chan in range(CH):
            coef_real = channel_mix[0, channel, other_chan]
            coef_imag = channel_mix[1, channel, other_chan]
            sum_real = sum_real + coef_real * moved_real[other_chan] - coef_imag * moved_imag[other_chan]
            sum_imag = sum_imag + coef_real * moved_imag[other_chan] + coef_imag * moved_real[other_chan]
        filt_real = azimuth_filter[0, channel]
        filt_imag = azimuth_filter[1, channel]
        rows_real.append(filt_real * sum_real - filt_imag * sum_imag)
        rows_imag.append(filt_real * sum_imag + filt_imag * sum_real)
    foc_real = settle(jnp.stack(rows_real))
    foc_imag = settle(jnp.stack(rows_imag))
    back_re, back_im = rounded_pair(GROUP_P, WINDOW, WINDOW, 1.0, 1.0 / math.sqrt(WINDOW))
    img_real = jnp.einsum('pf,crf->cpr', back_re, foc_real) - jnp.einsum('pf,crf->cpr', back_im, foc_imag)
    img_imag = jnp.einsum('pf,crf->cpr', back_re, foc_imag) + jnp.einsum('pf,crf->cpr', back_im, foc_real)
    return jnp.stack([img_real, img_imag]).astype(jnp.bfloat16)

def reference(echoes, range_phase, offsets, tap_weights, channel_mix, azimuth_filter):
    grouped = echoes.reshape(2, CH, N_BLK, GROUP_P, NR).transpose(2, 0, 1, 3, 4)
    compressed = lax.map(lambda group: compress(group, range_phase), grouped)
    following = jnp.concatenate([compressed[1:, :, :, :INTERSECTION], jnp.zeros_like(compressed[:1, :, :, :INTERSECTION])], axis=0)
    windows = jnp.concatenate([compressed, following], axis=3)
    images = lax.map(lambda group: focus(group, offsets, tap_weights, channel_mix, azimuth_filter), windows)
    return images.transpose(1, 2, 0, 3, 4).reshape(2, CH, PULSES, NR)
```

```python
import functools
import math

import jax
import jax.numpy as jnp
import numpy as np
from jax import lax
from jax.experimental import pallas as pl
from jax.experimental.pallas import tpu as pltpu
from jax.sharding import PartitionSpec as P

R1 = 128
LANES = 128
MARG = 64
F32 = jnp.float32
BF16 = jnp.bfloat16
MESH = pl.DeviceIdType.MESH


def phases(rows, cols, length):
    product = np.outer(rows, cols) % length
    angle = product.astype(np.float64) * (2.0 * math.pi / length)
    return np.cos(angle), np.sin(angle)


def range_table():
    index = np.arange(R1)
    cosine, sine = phases(index, index, R1)
    return np.block([[cosine, -sine], [sine, cosine]]).astype(BF16)


def twist_tables(range_bins):
    cosine, sine = phases(np.arange(R1), np.arange(range_bins // R1), range_bins)
    scale = 1.0 / math.sqrt(range_bins)
    return np.stack([cosine * scale, sine * scale]).astype(np.float32)


def doppler_table(pulse_of_row, wide):
    senders, pulses = pulse_of_row.shape
    cosine, sine = phases(pulse_of_row.reshape(-1), np.arange(wide), wide)
    keep = (pulse_of_row.reshape(-1) >= 0)[:, None] / math.sqrt(wide)
    real = (cosine * keep).reshape(senders, 1, pulses, wide)
    imag = (-sine * keep).reshape(senders, 1, pulses, wide)
    from_real = np.concatenate([real, imag], axis=3)
    from_imag = np.concatenate([-imag, real], axis=3)
    return np.concatenate([from_real, from_imag], axis=1).reshape(-1, 2 * wide).astype(BF16)


def image_table(pulses, wide):
    cosine, sine = phases(np.arange(pulses), np.arange(wide), wide)
    scale = 1.0 / math.sqrt(wide)
    return (np.block([[cosine, -sine], [sine, cosine]]) * scale).astype(BF16)


def cos_sin(angle):
    y = angle * 0.25
    z = y * y
    sine = y * (1 + z * (-1 / 6 + z * (1 / 120 + z * (-1 / 5040 + z * (1 / 362880 - z / 39916800)))))
    vers = z * (0.5 + z * (-1 / 24 + z * (1 / 720 + z * (-1 / 40320 + z / 3628800))))
    for _ in range(2):
        sine, vers = 2 * sine * (1 - vers), 2 * sine * sine
    return 1 - vers, sine


def kernel(
    n, pulses, wide, tiles,
    echo_ref, phase_ref, offs_ref, taps_ref, mix_ref, filt_ref,
    rng_ref, twist_ref, fwd_ref, back_ref,
    out_ref,
    raw, spec, part, comp, send, recv, halo, dop, foc, img, phase, coef,
    send_sem, first_sem, tile_sem, halo_send, halo_recv,
):
    me = lax.axis_index("dev")
    channels = echo_ref.shape[1]
    taps = taps_ref.shape[0]
    rows = 2 * pulses
    block = tiles * LANES
    group_pulses = out_ref.shape[2]

    barrier = pltpu.get_barrier_semaphore()

    @pl.loop(1, n)
    def _(i):
        pl.semaphore_signal(
            barrier, inc=1, device_id={"dev": lax.rem(me + i, n)}, device_id_type=MESH
        )

    cosine, sine = cos_sin(phase_ref[...])
    phase[0] = cosine
    phase[1] = sine

    def range_channel(c):
        for ri in range(2):
            for k in range(R1):
                raw[ri, k * pulses : (k + 1) * pulses, :] = echo_ref[
                    ri, c, :, k * LANES : (k + 1) * LANES
                ].astype(F32)
        for q in range(pulses):
            real = raw[0, pl.ds(q, R1, stride=pulses), :]
            imag = raw[1, pl.ds(q, R1, stride=pulses), :]
            cosine = phase[0]
            sine = phase[1]
            at = slice(q * LANES, (q + 1) * LANES)
            spec[:R1, at] = (real * cosine - imag * sine).astype(BF16)
            spec[R1:, at] = (real * sine + imag * cosine).astype(BF16)
        half = 4
        for q0 in range(0, pulses, half):
            span = slice(q0 * LANES, (q0 + half) * LANES)
            section = jnp.dot(rng_ref[...], spec[:, span], preferred_element_type=F32)
            for q in range(half):
                real = section[:R1, q * LANES : (q + 1) * LANES]
                imag = section[R1:, q * LANES : (q + 1) * LANES]
                at = slice((q0 + q) * LANES, (q0 + q + 1) * LANES)
                part[at, :LANES] = (real * twist_ref[0] - imag * twist_ref[1]).astype(BF16)
                part[at, LANES:] = (real * twist_ref[1] + imag * twist_ref[0]).astype(BF16)
            result = lax.dot_general(
                rng_ref[...], part[span, :], (((1,), (1,)), ((), ())), preferred_element_type=F32
            )
            for q in range(half):
                at = slice(q * LANES, (q + 1) * LANES)
                comp[pl.ds(q0 + q, R1, stride=rows), :] = result[:R1, at]
                comp[pl.ds(pulses + q0 + q, R1, stride=rows), :] = result[R1:, at]
        for first in range(0, R1, 16):
            piece = comp[first * rows : (first + 16) * rows, :]
            send[c, first : first + 16] = piece.reshape(16, rows, LANES).astype(BF16)

    def first_copy(c, peer):
        return pltpu.make_async_remote_copy(
            src_ref=send.at[c, peer * tiles],
            dst_ref=recv.at[0, c, me],
            send_sem=send_sem,
            recv_sem=first_sem,
            device_id={"dev": peer},
            device_id_type=MESH,
        )

    def tile_copy(t, peer):
        return pltpu.make_async_remote_copy(
            src_ref=send.at[:, peer * tiles + t],
            dst_ref=recv.at[t, :, me],
            send_sem=send_sem,
            recv_sem=tile_sem.at[t],
            device_id={"dev": peer},
            device_id_type=MESH,
        )

    @pl.loop(0, channels)
    def _(c):
        range_channel(c)

        @pl.when(c == 0)
        def _():
            pl.semaphore_wait(barrier, n - 1)

        @pl.loop(1, n)
        def _(i):
            first_copy(c, lax.rem(me + i, n)).start()

        recv[0, c, me] = send[c, me * tiles]

    @pl.loop(1, tiles)
    def _(i):
        t = tiles - i

        @pl.loop(1, n)
        def _(j):
            tile_copy(t, lax.rem(me + j, n)).start()

        for c in range(channels):
            recv[t, c, me] = send[c, me * tiles + t]

    for c in range(channels):
        for ri in range(2):
            other = mix_ref[1 - ri, c]
            sign = -1.0 if ri == 0 else 1.0
            coef[ri, c] = (
                filt_ref[0, c : c + 1, :] * mix_ref[ri, c]
                + sign * filt_ref[1, c : c + 1, :] * other
            )

    def spectra(load, first, count):
        window = jnp.concatenate(
            [load(c).reshape(n * rows, LANES)[:, :count] for c in range(channels)], axis=1
        )
        result = lax.dot_general(
            window, fwd_ref[...], (((0,), (0,)), ((), ())), preferred_element_type=F32
        ).astype(BF16).astype(F32)
        for c in range(channels):
            dop[c, pl.ds(first, count), :] = result[c * count : (c + 1) * count]

    def focus_rows(first, start, stop):
        @pl.loop(start, stop)
        def _(step):
            row = pl.multiple_of(step * 16, 16)
            base = pl.multiple_of(first + row, 16)
            near = dop.at[:, pl.ds(base, 24), :]
            for f in range(wide // LANES):
                at = slice(f * LANES, (f + 1) * LANES)
                moved = []
                for d in range(channels):
                    pair = []
                    for ri in range(2):
                        where = slice(ri * wide + f * LANES, ri * wide + (f + 1) * LANES)
                        total = near[d, :16, where] * taps_ref[0:1, at]
                        for j in range(1, taps):
                            total = total + near[d, j : j + 16, where] * taps_ref[j : j + 1, at]
                        pair.append(total)
                    moved.append(pair)
                for c in range(channels):
                    real = imag = None
                    for d in range(channels):
                        re, im = moved[d]
                        cre = coef[0, c, d : d + 1, at]
                        cim = coef[1, c, d : d + 1, at]
                        new_real = cre * re - cim * im
                        new_imag = cre * im + cim * re
                        real = new_real if d == 0 else real + new_real
                        imag = new_imag if d == 0 else imag + new_imag
                    foc[c, pl.ds(row, 16), at] = real.astype(BF16)
                    foc[c, pl.ds(row, 16), wide + f * LANES : wide + (f + 1) * LANES] = imag.astype(BF16)

    def image(slot, count):
        columns = foc[:, :count, :].reshape(channels * count, 2 * wide)
        result = lax.dot_general(
            back_ref[...], columns, (((1,), (1,)), ((), ())), preferred_element_type=F32
        ).astype(BF16)
        for c in range(channels):
            img[slot, c, :, :count] = result[:, c * count : (c + 1) * count]

    def pick(t):
        target = offs_ref[pl.ds(t, 1), :] + lax.broadcasted_iota(jnp.int32, (1, LANES), 1)
        source = lax.broadcasted_iota(jnp.int32, (2 * LANES, LANES), 0)
        onehot = jnp.where(source == target, 1.0, 0.0).astype(BF16)
        for c in range(channels):
            both = jnp.concatenate([img[t, c], img[t + 1, c]], axis=1)
            result = jnp.dot(both, onehot, preferred_element_type=F32).astype(BF16)
            for ri in range(2):
                out_ref[ri, c, :, pl.ds(pl.multiple_of(t * LANES, LANES), LANES)] = result[
                    ri * group_pulses : (ri + 1) * group_pulses
                ]

    def wait_bytes(sem, ref):
        pltpu.make_async_copy(ref, ref, sem).wait()

    wait_bytes(first_sem, recv.at[0, :, : n - 1])
    dop[:, block + MARG :, :] = jnp.zeros_like(dop[:, block + MARG :, :])
    img[tiles, :, :, MARG:] = jnp.zeros_like(img[tiles, :, :, MARG:])

    halo_copy = pltpu.make_async_remote_copy(
        src_ref=recv.at[0],
        dst_ref=halo,
        send_sem=halo_send,
        recv_sem=halo_recv,
        device_id={"dev": lax.rem(me + n - 1, n)},
        device_id_type=MESH,
    )

    @pl.when(me > 0)
    def _():
        halo_copy.start()

    spectra(lambda c: recv[0, c], 0, LANES)

    @pl.when(me < n - 1)
    def _():
        halo_copy.wait_recv()

    @pl.when(me == n - 1)
    def _():
        halo[...] = jnp.zeros_like(halo)

    spectra(lambda c: halo[c], block, MARG)
    focus_rows(block, 0, MARG // 16)
    image(tiles, MARG)

    @pl.loop(1, tiles)
    def _(i):
        t = tiles - i
        wait_bytes(tile_sem.at[t], recv.at[t, :, : n - 1])
        first = pl.multiple_of(t * LANES, LANES)
        spectra(lambda c: recv[t, c], first, LANES)
        focus_rows(first, 0, LANES // 16)
        image(t, LANES)
        pick(t)

    focus_rows(0, 0, LANES // 16)
    image(0, LANES)
    pick(0)

    wait_bytes(send_sem, send.at[:, : (n - 1) * tiles])

    @pl.when(me > 0)
    def _():
        halo_copy.wait_send()


def body(echoes, range_phase, offsets, tap_weights, channel_mix, azimuth_filter):
    n = lax.axis_size("dev")
    groups = lax.axis_size("blk")
    channels, own, range_bins = echoes.shape[1:]
    block = range_bins // n
    tiles = block // LANES
    wide = tap_weights.shape[1]
    group_pulses = own * n
    pulse_of_row = np.arange(group_pulses).reshape(n, own)
    if groups > 1:
        following = lax.ppermute(echoes, "blk", [(i, i - 1) for i in range(1, groups)])
        echoes = jnp.concatenate([echoes, following], axis=2)
        later = pulse_of_row + group_pulses
        later = np.where(later < wide, later, -1)
        pulse_of_row = np.concatenate([pulse_of_row, later], axis=1)
    pulses = echoes.shape[2]
    rows = 2 * pulses
    vmem = pl.BlockSpec(memory_space=pltpu.VMEM)
    call = pl.pallas_call(
        functools.partial(kernel, n, pulses, wide, tiles),
        out_shape=jax.ShapeDtypeStruct((2, channels, group_pulses, block), BF16),
        in_specs=[vmem] * 10,
        out_specs=vmem,
        scratch_shapes=[
            pltpu.VMEM((2, R1 * pulses, LANES), F32),
            pltpu.VMEM((2 * R1, pulses * LANES), BF16),
            pltpu.VMEM((pulses * LANES, 2 * LANES), BF16),
            pltpu.VMEM((R1 * rows, LANES), F32),
            pltpu.VMEM((channels, R1, rows, LANES), BF16),
            pltpu.VMEM((tiles, channels, n, rows, LANES), BF16),
            pltpu.VMEM((channels, n, rows, LANES), BF16),
            pltpu.VMEM((channels, block + MARG + 16, 2 * wide), F32),
            pltpu.VMEM((channels, LANES, 2 * wide), BF16),
            pltpu.VMEM((tiles + 1, channels, 2 * group_pulses, LANES), BF16),
            pltpu.VMEM((2, R1, LANES), F32),
            pltpu.VMEM((2, channels, channels, wide), F32),
            pltpu.SemaphoreType.DMA,
            pltpu.SemaphoreType.DMA,
            pltpu.SemaphoreType.DMA((tiles,)),
            pltpu.SemaphoreType.DMA,
            pltpu.SemaphoreType.DMA,
        ],
        compiler_params=pltpu.CompilerParams(
            collective_id=0, has_side_effects=True, vmem_limit_bytes=56 * 1024 * 1024
        ),
        cost_estimate=pl.CostEstimate(
            flops=6 * 10**9, bytes_accessed=8 * 2**20, transcendentals=0
        ),
        name="focus",
    )
    return call(
        echoes,
        range_phase.reshape(R1, range_bins // R1),
        offsets.reshape(tiles, LANES),
        tap_weights,
        channel_mix,
        azimuth_filter,
        jnp.asarray(range_table()),
        jnp.asarray(twist_tables(range_bins)),
        jnp.asarray(doppler_table(pulse_of_row, wide)),
        jnp.asarray(image_table(group_pulses, wide)),
    )


def solution(mesh):
    in_specs = (P(None, None, ("blk", "dev"), None), P(), P("dev"), P(), P(), P())
    out_specs = P(None, None, "blk", "dev")
    return jax.shard_map(body, mesh=mesh, in_specs=in_specs, out_specs=out_specs, check_vma=False)
```

```python
import functools
import math

import jax
import jax.numpy as jnp
import numpy as np
from jax import lax
from jax.experimental import pallas as pl
from jax.experimental.pallas import tpu as pltpu
from jax.sharding import PartitionSpec as P

R1 = 128
LANES = 128
MARG = 64
PLANE = 8
F32 = jnp.float32
BF16 = jnp.bfloat16
MESH = pl.DeviceIdType.MESH


def phases(rows, cols, length):
    product = np.outer(rows, cols) % length
    angle = product.astype(np.float64) * (2.0 * math.pi / length)
    return np.cos(angle), np.sin(angle)


def range_table():
    index = np.arange(R1)
    cosine, sine = phases(index, index, R1)
    return np.block([[cosine, -sine], [sine, cosine]]).astype(BF16)


def twist_tables(range_bins):
    cosine, sine = phases(np.arange(R1), np.arange(range_bins // R1), range_bins)
    scale = 1.0 / math.sqrt(range_bins)
    return np.stack([cosine * scale, sine * scale]).astype(np.float32)


def doppler_table(pulse_of_row, wide):
    senders, pulses = pulse_of_row.shape
    cosine, sine = phases(pulse_of_row.reshape(-1), np.arange(wide), wide)
    keep = (pulse_of_row.reshape(-1) >= 0)[:, None] / math.sqrt(wide)
    real = (cosine * keep).reshape(senders, 1, pulses, wide)
    imag = (-sine * keep).reshape(senders, 1, pulses, wide)
    from_real = np.concatenate([real, imag], axis=3)
    from_imag = np.concatenate([-imag, real], axis=3)
    return np.concatenate([from_real, from_imag], axis=1).reshape(-1, 2 * wide).astype(BF16)


def image_table(pulses, wide):
    cosine, sine = phases(np.arange(pulses), np.arange(wide), wide)
    scale = 1.0 / math.sqrt(wide)
    return (np.block([[cosine, -sine], [sine, cosine]]) * scale).astype(BF16)


def cos_sin(angle):
    y = angle * 0.25
    z = y * y
    sine = y * (1 + z * (-1 / 6 + z * (1 / 120 + z * (-1 / 5040 + z * (1 / 362880 - z / 39916800)))))
    vers = z * (0.5 + z * (-1 / 24 + z * (1 / 720 + z * (-1 / 40320 + z / 3628800))))
    for _ in range(2):
        sine, vers = 2 * sine * (1 - vers), 2 * sine * sine
    return 1 - vers, sine


def kernel(
    n, pulses, wide, tiles, edges,
    echo_ref, phase_ref, offs_ref, taps_ref, mix_ref, filt_ref,
    rng_ref, twist_ref, fwd_ref, back_ref,
    out_ref,
    raw, spec, part, comp, send, recv, halo, dop, foc, early, img, phase, coef,
    send_sem, first_sem, tile_sem, halo_send, halo_recv, edge_send,
):
    me = lax.axis_index("dev")
    channels = echo_ref.shape[1]
    taps = taps_ref.shape[0]
    rows = 2 * pulses
    block = tiles * LANES
    group_pulses = out_ref.shape[2]

    stride = next(s for s in (11, 7, 5, 3, 1) if math.gcd(s, n) == 1)

    def peer_of(i):
        return lax.rem(me + stride * i, n)

    barrier = pltpu.get_barrier_semaphore()

    @pl.loop(1, n)
    def _(i):
        pl.semaphore_signal(
            barrier, inc=1, device_id={"dev": lax.rem(me + i, n)}, device_id_type=MESH
        )

    cosine, sine = cos_sin(phase_ref[...])
    phase[0] = cosine
    phase[1] = sine

    def range_channel(c):
        for ri in range(2):
            for k in range(R1):
                raw[ri, k * pulses : (k + 1) * pulses, :] = echo_ref[
                    ri, c, :, k * LANES : (k + 1) * LANES
                ].astype(F32)
        for q in range(pulses):
            real = raw[0, pl.ds(q, R1, stride=pulses), :]
            imag = raw[1, pl.ds(q, R1, stride=pulses), :]
            cosine = phase[0]
            sine = phase[1]
            at = slice(q * LANES, (q + 1) * LANES)
            spec[:R1, at] = (real * cosine - imag * sine).astype(BF16)
            spec[R1:, at] = (real * sine + imag * cosine).astype(BF16)
        half = 4
        for q0 in range(0, pulses, half):
            span = slice(q0 * LANES, (q0 + half) * LANES)
            section = jnp.dot(rng_ref[...], spec[:, span], preferred_element_type=F32)
            for q in range(half):
                real = section[:R1, q * LANES : (q + 1) * LANES]
                imag = section[R1:, q * LANES : (q + 1) * LANES]
                at = slice((q0 + q) * LANES, (q0 + q + 1) * LANES)
                part[at, :LANES] = (real * twist_ref[0] - imag * twist_ref[1]).astype(BF16)
                part[at, LANES:] = (real * twist_ref[1] + imag * twist_ref[0]).astype(BF16)
            result = lax.dot_general(
                rng_ref[...], part[span, :], (((1,), (1,)), ((), ())), preferred_element_type=F32
            )
            for q in range(half):
                at = slice(q * LANES, (q + 1) * LANES)
                comp[pl.ds(q0 + q, R1, stride=rows), :] = result[:R1, at]
                comp[pl.ds(pulses + q0 + q, R1, stride=rows), :] = result[R1:, at]
        for first in range(0, R1, 16):
            piece = comp[first * rows : (first + 16) * rows, :]
            send[c, first : first + 16] = piece.reshape(16, rows, LANES).astype(BF16)

    def first_copy(c, peer):
        return pltpu.make_async_remote_copy(
            src_ref=send.at[c, peer * tiles],
            dst_ref=recv.at[0, c, me],
            send_sem=send_sem,
            recv_sem=first_sem,
            device_id={"dev": peer},
            device_id_type=MESH,
        )

    def tile_copy(t, peer):
        return pltpu.make_async_remote_copy(
            src_ref=send.at[:, peer * tiles + t],
            dst_ref=recv.at[t, :, me],
            send_sem=send_sem,
            recv_sem=tile_sem.at[t],
            device_id={"dev": peer},
            device_id_type=MESH,
        )

    @pl.loop(0, channels)
    def _(c):
        range_channel(c)

        @pl.when(c == 0)
        def _():
            pl.semaphore_wait(barrier, n - 1)

        @pl.loop(1, n)
        def _(i):
            first_copy(c, peer_of(i)).start()

        recv[0, c, me] = send[c, me * tiles]

    def edge_copy(b):
        return pltpu.make_async_remote_copy(
            src_ref=send.at[:, b * tiles],
            dst_ref=halo.at[:, me],
            send_sem=edge_send,
            recv_sem=halo_recv,
            device_id={"dev": b - 1},
            device_id_type=MESH,
        )

    for b in edges:
        @pl.when(me != b - 1)
        def _():
            edge_copy(b).start()

        @pl.when(me == b - 1)
        def _():
            for c in range(channels):
                halo[c, me] = send[c, b * tiles]

    @pl.loop(1, tiles)
    def _(i):
        t = tiles - i

        @pl.loop(1, n)
        def _(j):
            tile_copy(t, peer_of(j)).start()

        for c in range(channels):
            recv[t, c, me] = send[c, me * tiles + t]

    for c in range(channels):
        for ri in range(2):
            other = mix_ref[1 - ri, c]
            sign = -1.0 if ri == 0 else 1.0
            coef[ri, c] = (
                filt_ref[0, c : c + 1, :] * mix_ref[ri, c]
                + sign * filt_ref[1, c : c + 1, :] * other
            )

    def spectra(load, first, count):
        window = jnp.concatenate(
            [load(c).reshape(n * rows, LANES)[:, :count] for c in range(channels)], axis=1
        )
        result = lax.dot_general(
            window, fwd_ref[...], (((0,), (0,)), ((), ())), preferred_element_type=F32
        ).astype(BF16).astype(F32)
        for c in range(channels):
            dop[c, pl.ds(first, count), :] = result[c * count : (c + 1) * count]

    def focus_rows(into, first, start, stop):
        @pl.loop(start, stop)
        def _(step):
            row = pl.multiple_of(step * 16, 16)
            base = pl.multiple_of(first + row, 16)
            near = dop.at[:, pl.ds(base, 24), :]
            for f in range(wide // LANES):
                at = slice(f * LANES, (f + 1) * LANES)
                moved = []
                for d in range(channels):
                    pair = []
                    for ri in range(2):
                        where = slice(ri * wide + f * LANES, ri * wide + (f + 1) * LANES)
                        total = near[d, :16, where] * taps_ref[0:1, at]
                        for j in range(1, taps):
                            total = total + near[d, j : j + 16, where] * taps_ref[j : j + 1, at]
                        pair.append(total)
                    moved.append(pair)
                for c in range(channels):
                    real = imag = None
                    for d in range(channels):
                        re, im = moved[d]
                        cre = coef[0, c, d : d + 1, at]
                        cim = coef[1, c, d : d + 1, at]
                        new_real = cre * re - cim * im
                        new_imag = cre * im + cim * re
                        real = new_real if d == 0 else real + new_real
                        imag = new_imag if d == 0 else imag + new_imag
                    into[c, pl.ds(row, 16), at] = real.astype(BF16)
                    into[c, pl.ds(row, 16), wide + f * LANES : wide + (f + 1) * LANES] = imag.astype(BF16)

    def image(source, slot, count):
        columns = source[:, :count, :].reshape(channels * count, 2 * wide)
        result = lax.dot_general(
            back_ref[...], columns, (((1,), (1,)), ((), ())), preferred_element_type=F32
        ).astype(BF16)
        for c in range(channels):
            img[slot, c, :, :count] = result[:, c * count : (c + 1) * count]

    def pick(t):
        target = offs_ref[pl.ds(t, 1), :] + lax.broadcasted_iota(jnp.int32, (1, LANES), 1)
        source = lax.broadcasted_iota(jnp.int32, (2 * LANES, LANES), 0)
        onehot = jnp.where(source == target, 1.0, 0.0).astype(BF16)
        for c in range(channels):
            both = jnp.concatenate([img[t, c], img[t + 1, c]], axis=1)
            result = jnp.dot(both, onehot, preferred_element_type=F32).astype(BF16)
            for ri in range(2):
                out_ref[ri, c, :, pl.ds(pl.multiple_of(t * LANES, LANES), LANES)] = result[
                    ri * group_pulses : (ri + 1) * group_pulses
                ]

    def wait_bytes(sem, ref):
        pltpu.make_async_copy(ref, ref, sem).wait()

    wait_bytes(first_sem, recv.at[0, :, : n - 1])
    dop[:, block + MARG :, :] = jnp.zeros_like(dop[:, block + MARG :, :])
    img[tiles, :, :, MARG:] = jnp.zeros_like(img[tiles, :, :, MARG:])

    halo_copy = pltpu.make_async_remote_copy(
        src_ref=recv.at[0],
        dst_ref=halo,
        send_sem=halo_send,
        recv_sem=halo_recv,
        device_id={"dev": lax.rem(me + n - 1, n)},
        device_id_type=MESH,
    )

    at_edge = lax.rem(me, PLANE) == 0
    before_edge = jnp.logical_or(lax.rem(me + 1, PLANE) == 0, me == n - 1)

    @pl.when(jnp.logical_not(at_edge))
    def _():
        halo_copy.start()

    spectra(lambda c: recv[0, c], 0, LANES)
    focus_rows(early, 0, 0, LANES // 16 - 1)

    @pl.when(jnp.logical_not(before_edge))
    def _():
        halo_copy.wait_recv()

    @pl.when(jnp.logical_and(before_edge, me < n - 1))
    def _():
        wait_bytes(halo_recv, halo.at[:, : n - 1])

    @pl.when(me == n - 1)
    def _():
        halo[...] = jnp.zeros_like(halo)

    spectra(lambda c: halo[c], block, MARG)
    focus_rows(foc, block, 0, MARG // 16)
    image(foc, tiles, MARG)

    @pl.loop(1, tiles)
    def _(i):
        t = tiles - i
        wait_bytes(tile_sem.at[t], recv.at[t, :, : n - 1])
        first = pl.multiple_of(t * LANES, LANES)
        spectra(lambda c: recv[t, c], first, LANES)
        focus_rows(foc, first, 0, LANES // 16)
        image(foc, t, LANES)
        pick(t)

    focus_rows(early, 0, LANES // 16 - 1, LANES // 16)
    image(early, 0, LANES)
    pick(0)

    wait_bytes(send_sem, send.at[:, : (n - 1) * tiles])

    @pl.when(jnp.logical_not(at_edge))
    def _():
        halo_copy.wait_send()

    for b in edges:
        @pl.when(me != b - 1)
        def _():
            edge_copy(b).wait_send()


def body(echoes, range_phase, offsets, tap_weights, channel_mix, azimuth_filter):
    n = lax.axis_size("dev")
    groups = lax.axis_size("blk")
    channels, own, range_bins = echoes.shape[1:]
    block = range_bins // n
    tiles = block // LANES
    wide = tap_weights.shape[1]
    group_pulses = own * n
    pulse_of_row = np.arange(group_pulses).reshape(n, own)
    if groups > 1:
        following = lax.ppermute(echoes, "blk", [(i, i - 1) for i in range(1, groups)])
        echoes = jnp.concatenate([echoes, following], axis=2)
        later = pulse_of_row + group_pulses
        later = np.where(later < wide, later, -1)
        pulse_of_row = np.concatenate([pulse_of_row, later], axis=1)
    pulses = echoes.shape[2]
    rows = 2 * pulses
    vmem = pl.BlockSpec(memory_space=pltpu.VMEM)
    call = pl.pallas_call(
        functools.partial(kernel, n, pulses, wide, tiles, tuple(range(PLANE, n, PLANE))),
        out_shape=jax.ShapeDtypeStruct((2, channels, group_pulses, block), BF16),
        in_specs=[vmem] * 10,
        out_specs=vmem,
        scratch_shapes=[
            pltpu.VMEM((2, R1 * pulses, LANES), F32),
            pltpu.VMEM((2 * R1, pulses * LANES), BF16),
            pltpu.VMEM((pulses * LANES, 2 * LANES), BF16),
            pltpu.VMEM((R1 * rows, LANES), F32),
            pltpu.VMEM((channels, R1, rows, LANES), BF16),
            pltpu.VMEM((tiles, channels, n, rows, LANES), BF16),
            pltpu.VMEM((channels, n, rows, LANES), BF16),
            pltpu.VMEM((channels, block + MARG + 16, 2 * wide), F32),
            pltpu.VMEM((channels, LANES, 2 * wide), BF16),
            pltpu.VMEM((channels, LANES, 2 * wide), BF16),
            pltpu.VMEM((tiles + 1, channels, 2 * group_pulses, LANES), BF16),
            pltpu.VMEM((2, R1, LANES), F32),
            pltpu.VMEM((2, channels, channels, wide), F32),
            pltpu.SemaphoreType.DMA,
            pltpu.SemaphoreType.DMA,
            pltpu.SemaphoreType.DMA((tiles,)),
            pltpu.SemaphoreType.DMA,
            pltpu.SemaphoreType.DMA,
            pltpu.SemaphoreType.DMA,
        ],
        compiler_params=pltpu.CompilerParams(
            collective_id=0, has_side_effects=True, vmem_limit_bytes=56 * 1024 * 1024
        ),
        cost_estimate=pl.CostEstimate(
            flops=6 * 10**9, bytes_accessed=8 * 2**20, transcendentals=0
        ),
        name="focus",
    )
    return call(
        echoes,
        range_phase.reshape(R1, range_bins // R1),
        offsets.reshape(tiles, LANES),
        tap_weights,
        channel_mix,
        azimuth_filter,
        jnp.asarray(range_table()),
        jnp.asarray(twist_tables(range_bins)),
        jnp.asarray(doppler_table(pulse_of_row, wide)),
        jnp.asarray(image_table(group_pulses, wide)),
    )


def solution(mesh):
    in_specs = (P(None, None, ("blk", "dev"), None), P(), P("dev"), P(), P(), P())
    out_specs = P(None, None, "blk", "dev")
    return jax.shard_map(body, mesh=mesh, in_specs=in_specs, out_specs=out_specs, check_vma=False)
```

```python
import functools
import math

import jax
import jax.numpy as jnp
import numpy as np
from jax import lax
from jax.experimental import pallas as pl
from jax.experimental.pallas import tpu as pltpu
from jax.sharding import PartitionSpec as P

R1 = 128
LANES = 128
MARG = 64
PLANE = 8
SPAN = 120
F32 = jnp.float32
BF16 = jnp.bfloat16
MESH = pl.DeviceIdType.MESH


def phases(rows, cols, length):
    product = np.outer(rows, cols) % length
    angle = product.astype(np.float64) * (2.0 * math.pi / length)
    return np.cos(angle), np.sin(angle)


def bin_order():
    place = np.arange(R1)
    return place // MARG * MARG + place % 8 * 8 + place % MARG // 8


def range_table(order):
    cosine, sine = phases(order, np.arange(R1), R1)
    return np.block([[cosine, -sine], [sine, cosine]]).astype(BF16)


def twist_tables(order, range_bins):
    cosine, sine = phases(order, np.arange(range_bins // R1), range_bins)
    scale = 1.0 / math.sqrt(range_bins)
    return np.stack([cosine * scale, sine * scale]).astype(np.float32)


def doppler_table(pulse_of_row, wide):
    senders, pulses = pulse_of_row.shape
    cosine, sine = phases(pulse_of_row.reshape(-1), np.arange(wide), wide)
    keep = (pulse_of_row.reshape(-1) >= 0)[:, None] / math.sqrt(wide)
    real = (cosine * keep).reshape(senders, 1, pulses, wide)
    imag = (-sine * keep).reshape(senders, 1, pulses, wide)
    from_real = np.concatenate([real, imag], axis=3)
    from_imag = np.concatenate([-imag, real], axis=3)
    return np.concatenate([from_real, from_imag], axis=1).reshape(-1, 2 * wide).astype(BF16)


def image_table(pulses, wide):
    cosine, sine = phases(np.arange(pulses), np.arange(wide), wide)
    scale = 1.0 / math.sqrt(wide)
    return (np.block([[cosine, -sine], [sine, cosine]]) * scale).astype(BF16)


def cos_sin(angle):
    y = angle * 0.25
    z = y * y
    sine = y * (1 + z * (-1 / 6 + z * (1 / 120 + z * (-1 / 5040 + z * (1 / 362880 - z / 39916800)))))
    vers = z * (0.5 + z * (-1 / 24 + z * (1 / 720 + z * (-1 / 40320 + z / 3628800))))
    for _ in range(2):
        sine, vers = 2 * sine * (1 - vers), 2 * sine * sine
    return 1 - vers, sine


def kernel(
    n, pulses, wide, tiles, edges,
    echo_ref, phase_ref, offs_ref, taps_ref, mix_ref, filt_ref,
    first_ref, second_ref, twist_ref, fwd_ref, back_ref,
    out_ref,
    raw, spec, part, comp, send, recv, halo, dop, foc, early, img, phase, coef,
    send_sem, first_sem, tile_sem, halo_send, halo_recv, edge_send,
):
    me = lax.axis_index("dev")
    channels = echo_ref.shape[1]
    taps = taps_ref.shape[0]
    rows = 2 * pulses
    block = tiles * LANES
    group_pulses = out_ref.shape[2]

    stride = next(s for s in (11, 7, 5, 3, 1) if math.gcd(s, n) == 1)

    def peer_of(i):
        return lax.rem(me + stride * i, n)

    barrier = pltpu.get_barrier_semaphore()

    @pl.loop(1, n)
    def _(i):
        pl.semaphore_signal(
            barrier, inc=1, device_id={"dev": lax.rem(me + i, n)}, device_id_type=MESH
        )

    cosine, sine = cos_sin(phase_ref[...])
    phase[0] = cosine
    phase[1] = sine

    def range_channel(c):
        for ri in range(2):
            for k in range(R1):
                raw[ri, k * pulses : (k + 1) * pulses, :] = echo_ref[
                    ri, c, :, k * LANES : (k + 1) * LANES
                ].astype(F32)
        for q in range(pulses):
            real = raw[0, pl.ds(q, R1, stride=pulses), :]
            imag = raw[1, pl.ds(q, R1, stride=pulses), :]
            cosine = phase[0]
            sine = phase[1]
            at = slice(q * LANES, (q + 1) * LANES)
            spec[:R1, at] = (real * cosine - imag * sine).astype(BF16)
            spec[R1:, at] = (real * sine + imag * cosine).astype(BF16)
        half = 4
        for q0 in range(0, pulses, half):
            span = slice(q0 * LANES, (q0 + half) * LANES)
            section = jnp.dot(first_ref[...], spec[:, span], preferred_element_type=F32)
            for q in range(half):
                real = section[:R1, q * LANES : (q + 1) * LANES]
                imag = section[R1:, q * LANES : (q + 1) * LANES]
                at = slice((q0 + q) * LANES, (q0 + q + 1) * LANES)
                part[at, :LANES] = (real * twist_ref[0] - imag * twist_ref[1]).astype(BF16)
                part[at, LANES:] = (real * twist_ref[1] + imag * twist_ref[0]).astype(BF16)
            result = lax.dot_general(
                second_ref[...], part[span, :], (((1,), (1,)), ((), ())), preferred_element_type=F32
            )
            for q in range(half):
                at = slice(q * LANES, (q + 1) * LANES)
                comp[pl.ds(q0 + q, R1, stride=rows), :] = result[:R1, at]
                comp[pl.ds(pulses + q0 + q, R1, stride=rows), :] = result[R1:, at]
        for first in range(0, R1, 16):
            piece = comp[first * rows : (first + 16) * rows, :]
            send[c, first : first + 16] = piece.reshape(16, rows, LANES).astype(BF16)

    def first_copy(c, peer):
        return pltpu.make_async_remote_copy(
            src_ref=send.at[c, peer * tiles],
            dst_ref=recv.at[0, c, me],
            send_sem=send_sem,
            recv_sem=first_sem,
            device_id={"dev": peer},
            device_id_type=MESH,
        )

    def tile_copy(t, peer):
        return pltpu.make_async_remote_copy(
            src_ref=send.at[:, peer * tiles + t],
            dst_ref=recv.at[t, :, me],
            send_sem=send_sem,
            recv_sem=tile_sem.at[t],
            device_id={"dev": peer},
            device_id_type=MESH,
        )

    @pl.loop(0, channels)
    def _(c):
        range_channel(c)

        @pl.when(c == 0)
        def _():
            pl.semaphore_wait(barrier, n - 1)

        @pl.loop(1, n)
        def _(i):
            first_copy(c, peer_of(i)).start()

        recv[0, c, me] = send[c, me * tiles]

    def edge_copy(b):
        return pltpu.make_async_remote_copy(
            src_ref=send.at[:, b * tiles],
            dst_ref=halo.at[:, me],
            send_sem=edge_send,
            recv_sem=halo_recv,
            device_id={"dev": b - 1},
            device_id_type=MESH,
        )

    for b in edges:
        @pl.when(me != b - 1)
        def _():
            edge_copy(b).start()

        @pl.when(me == b - 1)
        def _():
            for c in range(channels):
                halo[c, me] = send[c, b * tiles]

    @pl.loop(1, tiles)
    def _(i):
        t = tiles - i

        @pl.loop(1, n)
        def _(j):
            tile_copy(t, peer_of(j)).start()

        for c in range(channels):
            recv[t, c, me] = send[c, me * tiles + t]

    for c in range(channels):
        for ri in range(2):
            other = mix_ref[1 - ri, c]
            sign = -1.0 if ri == 0 else 1.0
            coef[ri, c] = (
                filt_ref[0, c : c + 1, :] * mix_ref[ri, c]
                + sign * filt_ref[1, c : c + 1, :] * other
            )

    def spectra(load, first, count):
        window = jnp.concatenate(
            [load(c).reshape(n * rows, LANES)[:, :count] for c in range(channels)], axis=1
        )
        result = lax.dot_general(
            window, fwd_ref[...], (((0,), (0,)), ((), ())), preferred_element_type=F32
        ).astype(BF16).astype(F32)
        for c in range(channels):
            for h in range(count // MARG):
                at = pl.multiple_of((first + h) * SPAN, 8)
                start = c * count + h * MARG
                dop[c, pl.ds(at, MARG), :] = result[start : start + MARG]

    def extend(b):
        here = dop.at[:, pl.ds(pl.multiple_of(b * SPAN, 8), SPAN), :]
        after = dop.at[:, pl.ds(pl.multiple_of((b + 1) * SPAN, 8), MARG), :]
        top = lax.broadcasted_iota(jnp.int32, (8, 2 * wide), 0) == 0
        for c in range(channels):
            for m in range(taps - 1):
                rows_here = slice(m * 8, m * 8 + 8)
                mixed = jnp.where(top, after[c, rows_here, :], here[c, rows_here, :])
                here[c, MARG + m * 8 : MARG + m * 8 + 8, :] = pltpu.roll(mixed, 7, 0)

    def focus_rows(into, first, start, stop):
        @pl.loop(start, stop)
        def _(step):
            row = pl.multiple_of(step * 16, 16)
            part_of = step // 4
            base = pl.multiple_of((first + part_of) * SPAN + (step - part_of * 4) * 16, 8)
            near = dop.at[:, pl.ds(base, 16 + 8 * (taps - 1)), :]
            for f in range(wide // LANES):
                at = slice(f * LANES, (f + 1) * LANES)
                moved = []
                for d in range(channels):
                    pair = []
                    for ri in range(2):
                        where = slice(ri * wide + f * LANES, ri * wide + (f + 1) * LANES)
                        total = near[d, :16, where] * taps_ref[0:1, at]
                        for j in range(1, taps):
                            total = total + near[d, 8 * j : 8 * j + 16, where] * taps_ref[j : j + 1, at]
                        pair.append(total)
                    moved.append(pair)
                for c in range(channels):
                    real = imag = None
                    for d in range(channels):
                        re, im = moved[d]
                        cre = coef[0, c, d : d + 1, at]
                        cim = coef[1, c, d : d + 1, at]
                        new_real = cre * re - cim * im
                        new_imag = cre * im + cim * re
                        real = new_real if d == 0 else real + new_real
                        imag = new_imag if d == 0 else imag + new_imag
                    into[c, pl.ds(row, 16), at] = real.astype(BF16)
                    into[c, pl.ds(row, 16), wide + f * LANES : wide + (f + 1) * LANES] = imag.astype(BF16)

    def image(source, slot, count):
        columns = source[:, :count, :].reshape(channels * count, 2 * wide)
        result = lax.dot_general(
            back_ref[...], columns, (((1,), (1,)), ((), ())), preferred_element_type=F32
        ).astype(BF16)
        for c in range(channels):
            img[slot, c, :, :count] = result[:, c * count : (c + 1) * count]

    def pick(t):
        target = offs_ref[pl.ds(t, 1), :] + lax.broadcasted_iota(jnp.int32, (1, LANES), 1)
        place = lax.broadcasted_iota(jnp.int32, (2 * LANES, LANES), 0)
        source = (place >> 6 << 6) + ((place & 7) << 3) + (place >> 3 & 7)
        onehot = jnp.where(source == target, 1.0, 0.0).astype(BF16)
        for c in range(channels):
            both = jnp.concatenate([img[t, c], img[t + 1, c]], axis=1)
            result = jnp.dot(both, onehot, preferred_element_type=F32).astype(BF16)
            for ri in range(2):
                out_ref[ri, c, :, pl.ds(pl.multiple_of(t * LANES, LANES), LANES)] = result[
                    ri * group_pulses : (ri + 1) * group_pulses
                ]

    def wait_bytes(sem, ref):
        pltpu.make_async_copy(ref, ref, sem).wait()

    wait_bytes(first_sem, recv.at[0, :, : n - 1])
    last = block // MARG
    end = (last + 1) * SPAN
    dop[:, end:, :] = jnp.zeros_like(dop[:, end:, :])
    img[tiles, :, :, MARG:] = jnp.zeros_like(img[tiles, :, :, MARG:])

    halo_copy = pltpu.make_async_remote_copy(
        src_ref=recv.at[0],
        dst_ref=halo,
        send_sem=halo_send,
        recv_sem=halo_recv,
        device_id={"dev": lax.rem(me + n - 1, n)},
        device_id_type=MESH,
    )

    at_edge = lax.rem(me, PLANE) == 0
    before_edge = jnp.logical_or(lax.rem(me + 1, PLANE) == 0, me == n - 1)

    @pl.when(jnp.logical_not(at_edge))
    def _():
        halo_copy.start()

    spectra(lambda c: recv[0, c], 0, LANES)
    extend(0)
    focus_rows(early, 0, 0, 4)

    @pl.when(jnp.logical_not(before_edge))
    def _():
        halo_copy.wait_recv()

    @pl.when(jnp.logical_and(before_edge, me < n - 1))
    def _():
        wait_bytes(halo_recv, halo.at[:, : n - 1])

    @pl.when(me == n - 1)
    def _():
        halo[...] = jnp.zeros_like(halo)

    spectra(lambda c: halo[c], last, MARG)
    extend(last)
    focus_rows(foc, last, 0, MARG // 16)
    image(foc, tiles, MARG)

    @pl.loop(1, tiles)
    def _(i):
        t = tiles - i
        wait_bytes(tile_sem.at[t], recv.at[t, :, : n - 1])
        first = t * (LANES // MARG)
        spectra(lambda c: recv[t, c], first, LANES)
        extend(first)
        extend(first + 1)
        focus_rows(foc, first, 0, LANES // 16)
        image(foc, t, LANES)
        pick(t)

    extend(1)
    focus_rows(early, 0, 4, 8)
    image(early, 0, LANES)
    pick(0)

    wait_bytes(send_sem, send.at[:, : (n - 1) * tiles])

    @pl.when(jnp.logical_not(at_edge))
    def _():
        halo_copy.wait_send()

    for b in edges:
        @pl.when(me != b - 1)
        def _():
            edge_copy(b).wait_send()


def body(echoes, range_phase, offsets, tap_weights, channel_mix, azimuth_filter):
    n = lax.axis_size("dev")
    groups = lax.axis_size("blk")
    channels, own, range_bins = echoes.shape[1:]
    block = range_bins // n
    tiles = block // LANES
    wide = tap_weights.shape[1]
    group_pulses = own * n
    pulse_of_row = np.arange(group_pulses).reshape(n, own)
    if groups > 1:
        following = lax.ppermute(echoes, "blk", [(i, i - 1) for i in range(1, groups)])
        echoes = jnp.concatenate([echoes, following], axis=2)
        later = pulse_of_row + group_pulses
        later = np.where(later < wide, later, -1)
        pulse_of_row = np.concatenate([pulse_of_row, later], axis=1)
    pulses = echoes.shape[2]
    rows = 2 * pulses
    vmem = pl.BlockSpec(memory_space=pltpu.VMEM)
    call = pl.pallas_call(
        functools.partial(kernel, n, pulses, wide, tiles, tuple(range(PLANE, n, PLANE))),
        out_shape=jax.ShapeDtypeStruct((2, channels, group_pulses, block), BF16),
        in_specs=[vmem] * 11,
        out_specs=vmem,
        scratch_shapes=[
            pltpu.VMEM((2, R1 * pulses, LANES), F32),
            pltpu.VMEM((2 * R1, pulses * LANES), BF16),
            pltpu.VMEM((pulses * LANES, 2 * LANES), BF16),
            pltpu.VMEM((R1 * rows, LANES), F32),
            pltpu.VMEM((channels, R1, rows, LANES), BF16),
            pltpu.VMEM((tiles, channels, n, rows, LANES), BF16),
            pltpu.VMEM((channels, n, rows, LANES), BF16),
            pltpu.VMEM((channels, (block // MARG + 1) * SPAN + MARG, 2 * wide), F32),
            pltpu.VMEM((channels, LANES, 2 * wide), BF16),
            pltpu.VMEM((channels, LANES, 2 * wide), BF16),
            pltpu.VMEM((tiles + 1, channels, 2 * group_pulses, LANES), BF16),
            pltpu.VMEM((2, R1, LANES), F32),
            pltpu.VMEM((2, channels, channels, wide), F32),
            pltpu.SemaphoreType.DMA,
            pltpu.SemaphoreType.DMA,
            pltpu.SemaphoreType.DMA((tiles,)),
            pltpu.SemaphoreType.DMA,
            pltpu.SemaphoreType.DMA,
            pltpu.SemaphoreType.DMA,
        ],
        compiler_params=pltpu.CompilerParams(
            collective_id=0, has_side_effects=True, vmem_limit_bytes=36 * 1024 * 1024
        ),
        cost_estimate=pl.CostEstimate(
            flops=6 * 10**9, bytes_accessed=8 * 2**20, transcendentals=0
        ),
        name="focus",
    )
    return call(
        echoes,
        range_phase.reshape(R1, range_bins // R1),
        offsets.reshape(tiles, LANES),
        tap_weights,
        channel_mix,
        azimuth_filter,
        jnp.asarray(range_table(bin_order())),
        jnp.asarray(range_table(np.arange(R1))),
        jnp.asarray(twist_tables(bin_order(), range_bins)),
        jnp.asarray(doppler_table(pulse_of_row, wide)),
        jnp.asarray(image_table(group_pulses, wide)),
    )


def solution(mesh):
    in_specs = (P(None, None, ("blk", "dev"), None), P(), P("dev"), P(), P(), P())
    out_specs = P(None, None, "blk", "dev")
    return jax.shard_map(body, mesh=mesh, in_specs=in_specs, out_specs=out_specs, check_vma=False)
```

```python
import functools
import math

import jax
import jax.numpy as jnp
import numpy as np
from jax import lax
from jax.experimental import pallas as pl
from jax.experimental.pallas import tpu as pltpu
from jax.sharding import PartitionSpec as P

R1 = 128
LANES = 128
MARG = 64
PLANE = 8
SPAN = 120
F32 = jnp.float32
BF16 = jnp.bfloat16
MESH = pl.DeviceIdType.MESH


def phases(rows, cols, length):
    product = np.outer(rows, cols) % length
    angle = product.astype(np.float64) * (2.0 * math.pi / length)
    return np.cos(angle), np.sin(angle)


def bin_order():
    place = np.arange(R1)
    return place // MARG * MARG + place % 8 * 8 + place % MARG // 8


def range_table(order):
    cosine, sine = phases(order, np.arange(R1), R1)
    return np.block([[cosine, -sine], [sine, cosine]]).astype(BF16)


def twist_tables(order, range_bins):
    cosine, sine = phases(order, np.arange(range_bins // R1), range_bins)
    scale = 1.0 / math.sqrt(range_bins)
    return np.stack([cosine * scale, sine * scale]).astype(np.float32)


def doppler_table(pulse_of_row, wide):
    senders, pulses = pulse_of_row.shape
    cosine, sine = phases(pulse_of_row.reshape(-1), np.arange(wide), wide)
    keep = (pulse_of_row.reshape(-1) >= 0)[:, None] / math.sqrt(wide)
    real = (cosine * keep).reshape(senders, 1, pulses, wide)
    imag = (-sine * keep).reshape(senders, 1, pulses, wide)
    from_real = np.concatenate([real, imag], axis=3)
    from_imag = np.concatenate([-imag, real], axis=3)
    return np.concatenate([from_real, from_imag], axis=1).reshape(-1, 2 * wide).astype(BF16)


def image_table(pulses, wide):
    cosine, sine = phases(np.arange(pulses), np.arange(wide), wide)
    scale = 1.0 / math.sqrt(wide)
    return (np.block([[cosine, -sine], [sine, cosine]]) * scale).astype(BF16)


def cos_sin(angle):
    y = angle * 0.25
    z = y * y
    sine = y * (1 + z * (-1 / 6 + z * (1 / 120 + z * (-1 / 5040 + z * (1 / 362880 - z / 39916800)))))
    vers = z * (0.5 + z * (-1 / 24 + z * (1 / 720 + z * (-1 / 40320 + z / 3628800))))
    for _ in range(2):
        sine, vers = 2 * sine * (1 - vers), 2 * sine * sine
    return 1 - vers, sine


def kernel(
    n, pulses, wide, tiles, edges,
    *refs,
):
    far, out_ref, held, rest = refs[:11], refs[11], refs[12:23], refs[23:]
    echo_ref, phase_ref, offs_ref, taps_ref, mix_ref, filt_ref = held[:6]
    first_ref, second_ref, twist_ref, fwd_ref, back_ref = held[6:]
    raw, spec, part, comp, send, recv, halo, dop, foc, early, img, phase, coef = rest[:13]
    send_sem, first_sem, tile_sem, halo_send, halo_recv, edge_send, echo_sem, load_sem = rest[13:]

    def load_echo(c):
        return pltpu.make_async_copy(far[0].at[:, c], held[0].at[:, c], echo_sem.at[c])

    def load(k):
        return pltpu.make_async_copy(far[k], held[k], load_sem.at[k])

    load(1).start()
    load_echo(0).start()
    for k in (6, 8, 7):
        load(k).start()
    for c in range(1, echo_ref.shape[1]):
        load_echo(c).start()
    for k in (9, 3, 4, 5, 10, 2):
        load(k).start()
    me = lax.axis_index("dev")
    channels = echo_ref.shape[1]
    taps = taps_ref.shape[0]
    rows = 2 * pulses
    block = tiles * LANES
    group_pulses = out_ref.shape[2]

    stride = next(s for s in (11, 7, 5, 3, 1) if math.gcd(s, n) == 1)

    def peer_of(i):
        return lax.rem(me + stride * i, n)

    barrier = pltpu.get_barrier_semaphore()

    @pl.loop(1, n)
    def _(i):
        pl.semaphore_signal(
            barrier, inc=1, device_id={"dev": lax.rem(me + i, n)}, device_id_type=MESH
        )

    load(1).wait()
    cosine, sine = cos_sin(phase_ref[...])
    phase[0] = cosine
    phase[1] = sine
    for k in (6, 7, 8):
        load(k).wait()

    def range_channel(c):
        for ri in range(2):
            for k in range(R1):
                raw[ri, k * pulses : (k + 1) * pulses, :] = echo_ref[
                    ri, c, :, k * LANES : (k + 1) * LANES
                ].astype(F32)
        for q in range(pulses):
            real = raw[0, pl.ds(q, R1, stride=pulses), :]
            imag = raw[1, pl.ds(q, R1, stride=pulses), :]
            cosine = phase[0]
            sine = phase[1]
            at = slice(q * LANES, (q + 1) * LANES)
            spec[:R1, at] = (real * cosine - imag * sine).astype(BF16)
            spec[R1:, at] = (real * sine + imag * cosine).astype(BF16)
        half = 4
        for q0 in range(0, pulses, half):
            span = slice(q0 * LANES, (q0 + half) * LANES)
            section = jnp.dot(first_ref[...], spec[:, span], preferred_element_type=F32)
            for q in range(half):
                real = section[:R1, q * LANES : (q + 1) * LANES]
                imag = section[R1:, q * LANES : (q + 1) * LANES]
                at = slice((q0 + q) * LANES, (q0 + q + 1) * LANES)
                part[at, :LANES] = (real * twist_ref[0] - imag * twist_ref[1]).astype(BF16)
                part[at, LANES:] = (real * twist_ref[1] + imag * twist_ref[0]).astype(BF16)
            result = lax.dot_general(
                second_ref[...], part[span, :], (((1,), (1,)), ((), ())), preferred_element_type=F32
            )
            for q in range(half):
                at = slice(q * LANES, (q + 1) * LANES)
                comp[pl.ds(q0 + q, R1, stride=rows), :] = result[:R1, at]
                comp[pl.ds(pulses + q0 + q, R1, stride=rows), :] = result[R1:, at]
        for first in range(0, R1, 16):
            piece = comp[first * rows : (first + 16) * rows, :]
            send[c, first : first + 16] = piece.reshape(16, rows, LANES).astype(BF16)

    def first_copy(c, peer):
        return pltpu.make_async_remote_copy(
            src_ref=send.at[c, peer * tiles],
            dst_ref=recv.at[0, c, me],
            send_sem=send_sem,
            recv_sem=first_sem,
            device_id={"dev": peer},
            device_id_type=MESH,
        )

    def tile_copy(t, peer):
        return pltpu.make_async_remote_copy(
            src_ref=send.at[:, peer * tiles + t],
            dst_ref=recv.at[t, :, me],
            send_sem=send_sem,
            recv_sem=tile_sem.at[t],
            device_id={"dev": peer},
            device_id_type=MESH,
        )

    @pl.loop(0, channels)
    def _(c):
        load_echo(c).wait()
        range_channel(c)

        @pl.when(c == 0)
        def _():
            pl.semaphore_wait(barrier, n - 1)

        @pl.loop(1, n)
        def _(i):
            first_copy(c, peer_of(i)).start()

        recv[0, c, me] = send[c, me * tiles]

    def edge_copy(b):
        return pltpu.make_async_remote_copy(
            src_ref=send.at[:, b * tiles],
            dst_ref=halo.at[:, me],
            send_sem=edge_send,
            recv_sem=halo_recv,
            device_id={"dev": b - 1},
            device_id_type=MESH,
        )

    for b in edges:
        @pl.when(me != b - 1)
        def _():
            edge_copy(b).start()

        @pl.when(me == b - 1)
        def _():
            for c in range(channels):
                halo[c, me] = send[c, b * tiles]

    @pl.loop(1, tiles)
    def _(i):
        t = tiles - i

        @pl.loop(1, n)
        def _(j):
            tile_copy(t, peer_of(j)).start()

        for c in range(channels):
            recv[t, c, me] = send[c, me * tiles + t]

    for k in (9, 3, 4, 5, 10, 2):
        load(k).wait()

    for c in range(channels):
        for ri in range(2):
            other = mix_ref[1 - ri, c]
            sign = -1.0 if ri == 0 else 1.0
            coef[ri, c] = (
                filt_ref[0, c : c + 1, :] * mix_ref[ri, c]
                + sign * filt_ref[1, c : c + 1, :] * other
            )

    def spectra(load, first, count):
        window = jnp.concatenate(
            [load(c).reshape(n * rows, LANES)[:, :count] for c in range(channels)], axis=1
        )
        result = lax.dot_general(
            window, fwd_ref[...], (((0,), (0,)), ((), ())), preferred_element_type=F32
        ).astype(BF16).astype(F32)
        for c in range(channels):
            for h in range(count // MARG):
                at = pl.multiple_of((first + h) * SPAN, 8)
                start = c * count + h * MARG
                dop[c, pl.ds(at, MARG), :] = result[start : start + MARG]

    def extend(b):
        here = dop.at[:, pl.ds(pl.multiple_of(b * SPAN, 8), SPAN), :]
        after = dop.at[:, pl.ds(pl.multiple_of((b + 1) * SPAN, 8), MARG), :]
        top = lax.broadcasted_iota(jnp.int32, (8, 2 * wide), 0) == 0
        for c in range(channels):
            for m in range(taps - 1):
                rows_here = slice(m * 8, m * 8 + 8)
                mixed = jnp.where(top, after[c, rows_here, :], here[c, rows_here, :])
                here[c, MARG + m * 8 : MARG + m * 8 + 8, :] = pltpu.roll(mixed, 7, 0)

    def focus_rows(into, first, start, stop):
        @pl.loop(start, stop)
        def _(step):
            row = pl.multiple_of(step * 16, 16)
            part_of = step // 4
            base = pl.multiple_of((first + part_of) * SPAN + (step - part_of * 4) * 16, 8)
            near = dop.at[:, pl.ds(base, 16 + 8 * (taps - 1)), :]
            for f in range(wide // LANES):
                at = slice(f * LANES, (f + 1) * LANES)
                moved = []
                for d in range(channels):
                    pair = []
                    for ri in range(2):
                        where = slice(ri * wide + f * LANES, ri * wide + (f + 1) * LANES)
                        total = near[d, :16, where] * taps_ref[0:1, at]
                        for j in range(1, taps):
                            total = total + near[d, 8 * j : 8 * j + 16, where] * taps_ref[j : j + 1, at]
                        pair.append(total)
                    moved.append(pair)
                for c in range(channels):
                    real = imag = None
                    for d in range(channels):
                        re, im = moved[d]
                        cre = coef[0, c, d : d + 1, at]
                        cim = coef[1, c, d : d + 1, at]
                        new_real = cre * re - cim * im
                        new_imag = cre * im + cim * re
                        real = new_real if d == 0 else real + new_real
                        imag = new_imag if d == 0 else imag + new_imag
                    into[c, pl.ds(row, 16), at] = real.astype(BF16)
                    into[c, pl.ds(row, 16), wide + f * LANES : wide + (f + 1) * LANES] = imag.astype(BF16)

    def image(source, slot, count):
        columns = source[:, :count, :].reshape(channels * count, 2 * wide)
        result = lax.dot_general(
            back_ref[...], columns, (((1,), (1,)), ((), ())), preferred_element_type=F32
        ).astype(BF16)
        for c in range(channels):
            img[slot, c, :, :count] = result[:, c * count : (c + 1) * count]

    def pick(t):
        target = offs_ref[pl.ds(t, 1), :] + lax.broadcasted_iota(jnp.int32, (1, LANES), 1)
        place = lax.broadcasted_iota(jnp.int32, (2 * LANES, LANES), 0)
        source = (place >> 6 << 6) + ((place & 7) << 3) + (place >> 3 & 7)
        onehot = jnp.where(source == target, 1.0, 0.0).astype(BF16)
        for c in range(channels):
            both = jnp.concatenate([img[t, c], img[t + 1, c]], axis=1)
            result = jnp.dot(both, onehot, preferred_element_type=F32).astype(BF16)
            for ri in range(2):
                out_ref[ri, c, :, pl.ds(pl.multiple_of(t * LANES, LANES), LANES)] = result[
                    ri * group_pulses : (ri + 1) * group_pulses
                ]

    def wait_bytes(sem, ref):
        pltpu.make_async_copy(ref, ref, sem).wait()

    wait_bytes(first_sem, recv.at[0, :, : n - 1])
    last = block // MARG
    end = (last + 1) * SPAN
    dop[:, end:, :] = jnp.zeros_like(dop[:, end:, :])
    img[tiles, :, :, MARG:] = jnp.zeros_like(img[tiles, :, :, MARG:])

    halo_copy = pltpu.make_async_remote_copy(
        src_ref=recv.at[0],
        dst_ref=halo,
        send_sem=halo_send,
        recv_sem=halo_recv,
        device_id={"dev": lax.rem(me + n - 1, n)},
        device_id_type=MESH,
    )

    at_edge = lax.rem(me, PLANE) == 0
    before_edge = jnp.logical_or(lax.rem(me + 1, PLANE) == 0, me == n - 1)

    @pl.when(jnp.logical_not(at_edge))
    def _():
        halo_copy.start()

    spectra(lambda c: recv[0, c], 0, LANES)
    extend(0)
    focus_rows(early, 0, 0, 4)

    @pl.when(jnp.logical_not(before_edge))
    def _():
        halo_copy.wait_recv()

    @pl.when(jnp.logical_and(before_edge, me < n - 1))
    def _():
        wait_bytes(halo_recv, halo.at[:, : n - 1])

    @pl.when(me == n - 1)
    def _():
        halo[...] = jnp.zeros_like(halo)

    spectra(lambda c: halo[c], last, MARG)
    extend(last)
    focus_rows(foc, last, 0, MARG // 16)
    image(foc, tiles, MARG)

    @pl.loop(1, tiles)
    def _(i):
        t = tiles - i
        wait_bytes(tile_sem.at[t], recv.at[t, :, : n - 1])
        first = t * (LANES // MARG)
        spectra(lambda c: recv[t, c], first, LANES)
        extend(first)
        extend(first + 1)
        focus_rows(foc, first, 0, LANES // 16)
        image(foc, t, LANES)
        pick(t)

    extend(1)
    focus_rows(early, 0, 4, 8)
    image(early, 0, LANES)
    pick(0)

    wait_bytes(send_sem, send.at[:, : (n - 1) * tiles])

    @pl.when(jnp.logical_not(at_edge))
    def _():
        halo_copy.wait_send()

    for b in edges:
        @pl.when(me != b - 1)
        def _():
            edge_copy(b).wait_send()


def body(echoes, range_phase, offsets, tap_weights, channel_mix, azimuth_filter):
    n = lax.axis_size("dev")
    groups = lax.axis_size("blk")
    channels, own, range_bins = echoes.shape[1:]
    block = range_bins // n
    tiles = block // LANES
    wide = tap_weights.shape[1]
    group_pulses = own * n
    pulse_of_row = np.arange(group_pulses).reshape(n, own)
    if groups > 1:
        following = lax.ppermute(echoes, "blk", [(i, i - 1) for i in range(1, groups)])
        echoes = jnp.concatenate([echoes, following], axis=2)
        later = pulse_of_row + group_pulses
        later = np.where(later < wide, later, -1)
        pulse_of_row = np.concatenate([pulse_of_row, later], axis=1)
    pulses = echoes.shape[2]
    rows = 2 * pulses
    vmem = pl.BlockSpec(memory_space=pltpu.VMEM)
    operands = (
        echoes,
        range_phase.reshape(R1, range_bins // R1),
        offsets.reshape(tiles, LANES),
        tap_weights,
        channel_mix,
        azimuth_filter,
        jnp.asarray(range_table(bin_order())),
        jnp.asarray(range_table(np.arange(R1))),
        jnp.asarray(twist_tables(bin_order(), range_bins)),
        jnp.asarray(doppler_table(pulse_of_row, wide)),
        jnp.asarray(image_table(group_pulses, wide)),
    )
    call = pl.pallas_call(
        functools.partial(kernel, n, pulses, wide, tiles, tuple(range(PLANE, n, PLANE))),
        out_shape=jax.ShapeDtypeStruct((2, channels, group_pulses, block), BF16),
        in_specs=[pl.BlockSpec(memory_space=pltpu.HBM)] * 11,
        out_specs=vmem,
        scratch_shapes=[pltpu.VMEM(a.shape, a.dtype) for a in operands]
        + [
            pltpu.VMEM((2, R1 * pulses, LANES), F32),
            pltpu.VMEM((2 * R1, pulses * LANES), BF16),
            pltpu.VMEM((pulses * LANES, 2 * LANES), BF16),
            pltpu.VMEM((R1 * rows, LANES), F32),
            pltpu.VMEM((channels, R1, rows, LANES), BF16),
            pltpu.VMEM((tiles, channels, n, rows, LANES), BF16),
            pltpu.VMEM((channels, n, rows, LANES), BF16),
            pltpu.VMEM((channels, (block // MARG + 1) * SPAN + MARG, 2 * wide), F32),
            pltpu.VMEM((channels, LANES, 2 * wide), BF16),
            pltpu.VMEM((channels, LANES, 2 * wide), BF16),
            pltpu.VMEM((tiles + 1, channels, 2 * group_pulses, LANES), BF16),
            pltpu.VMEM((2, R1, LANES), F32),
            pltpu.VMEM((2, channels, channels, wide), F32),
            pltpu.SemaphoreType.DMA,
            pltpu.SemaphoreType.DMA,
            pltpu.SemaphoreType.DMA((tiles,)),
            pltpu.SemaphoreType.DMA,
            pltpu.SemaphoreType.DMA,
            pltpu.SemaphoreType.DMA,
            pltpu.SemaphoreType.DMA((channels,)),
            pltpu.SemaphoreType.DMA((11,)),
        ],
        compiler_params=pltpu.CompilerParams(
            collective_id=0, has_side_effects=True, vmem_limit_bytes=56 * 1024 * 1024
        ),
        cost_estimate=pl.CostEstimate(
            flops=6 * 10**9, bytes_accessed=8 * 2**20, transcendentals=0
        ),
        name="focus",
    )
    return call(*operands)


def solution(mesh):
    in_specs = (P(None, None, ("blk", "dev"), None), P(), P("dev"), P(), P(), P())
    out_specs = P(None, None, "blk", "dev")
    return jax.shard_map(body, mesh=mesh, in_specs=in_specs, out_specs=out_specs, check_vma=False)
```
